32 devices in a mesh: rows: 16 (over z, y, x), blk: 2 (over core).
Axes of the slice: x: 2, y: 2, z: 4, core: 2. Of those that a mesh axis runs over, the one named last changes fastest.
Arguments:
- inputs: bfloat16 [16384, 440], P('rows'), may hold values from -6 to 6
- proj: bfloat16 [4, 440, 512], P('blk'), may hold values from -0.25 to 0.25
- phase: bfloat16 [4, 512], P('blk'), may hold values from -3.140625 to 3.140625
- targets: bfloat16 [16384, 1024], P('rows', 'blk'), may hold values from -6 to 6
Outputs:
- coefs: float32 [4, 512, 1024], P(None, None, 'blk')
- residual: float32 [16384, 1024], P('rows', 'blk')
The draws below stay inside these ranges and needn't reach their ends.
All inputs are finite; a program needn't handle non-finite values.
Results may differ from the reference program's by a relative error of at most 0.0035.
The reference program's roundings to bfloat16 on the way count: a program that leaves them out, or rounds other values in their place, can miss the bound.
Values may be sent and summed in bfloat16 or wider, within the bound.
No kernel may reach another device: no remote copies, remote signals or barrier semaphores. Data moves between devices by JAX's collectives and lax.ppermute only.
A program may use at most 128 MiB of HBM per device.

```python
import math
import jax
import jax.numpy as jnp
from jax import lax

DIN = 440
F = 512
ROWS = 16384
NBLK = 4
TGT = 1024


def shard_levels(stream_key, extent, split, smallest, top_value):
    def one(position, parts):
        heights = jax.random.uniform(jax.random.fold_in(jax.random.fold_in(stream_key, 6), position), (parts,), jnp.float32, smallest / len(split), top_value / len(split))
        return jnp.repeat(jnp.exp(heights), extent[position] // parts).reshape((-1,) + (1,) * (len(extent) - position - 1))

    gain = one(*split[0])
    for cut in split[1:]:
        gain = gain * one(*cut)
    return gain


def centred(own_key, shape, width, bound, cuts=(), kind=jnp.bfloat16):
    result = width * jax.random.normal(own_key, shape, jnp.float32)
    if cuts:
        result = result * shard_levels(own_key, shape, cuts, -0.22, 0.18)
    return jnp.clip(result, -bound, bound).astype(kind)


def setup_inputs(seed: int = 0) -> dict:
    arg_keys = jax.random.split(jax.random.key(seed), 5)
    inputs = centred(arg_keys[0], (ROWS, DIN), 1.0, 6.0, ((0, 16),))
    proj = centred(arg_keys[1], (NBLK, DIN, F), DIN ** -0.5, 0.25, ((0, 2),))
    phase = jnp.clip(jax.random.uniform(arg_keys[2], (NBLK, F), jnp.float32, -3.140625, 3.140625), -3.140625, 3.140625).astype(jnp.bfloat16)
    targets = centred(arg_keys[3], (ROWS, TGT), 1.0, 6.0, ((0, 16), (1, 2)))
    return dict(inputs=inputs, proj=proj, phase=phase, targets=targets)


ridge = 0.05

def features(inputs, weights, shift):
    pre = jnp.dot(inputs.astype(jnp.float32), weights.astype(jnp.float32), preferred_element_type=jnp.float32) + shift.astype(jnp.float32)
    return (jnp.cos(pre) * (1.0 / math.sqrt(ROWS))).astype(jnp.bfloat16)

def reference(inputs, proj, phase, targets):
    identity_mat = jnp.eye(F, dtype=jnp.float32)
    factor_list = []
    for block in range(NBLK):
        feats = features(inputs, proj[block], phase[block])
        gram = lax.dot_general(feats.astype(jnp.float32), feats.astype(jnp.float32), (((0,), (0,)), ((), ())), preferred_element_type=jnp.float32)
        factor_list.append(jnp.linalg.cholesky(gram + ridge * identity_mat))
    residual = targets.astype(jnp.float32)
    coef_list = []
    for block in range(NBLK):
        feats = features(inputs, proj[block], phase[block])
        corr = lax.dot_general(feats.astype(jnp.float32), residual.astype(jnp.bfloat16).astype(jnp.float32), (((0,), (0,)), ((), ())), preferred_element_type=jnp.float32)
        delta = jax.scipy.linalg.cho_solve((factor_list[block], True), corr)
        coef_list.append(delta)
        residual = residual - jnp.dot(feats.astype(jnp.float32), delta.astype(jnp.bfloat16).astype(jnp.float32), preferred_element_type=jnp.float32)
    return (jnp.stack(coef_list), residual)
```

```python
import functools
import math

import jax
import jax.numpy as jnp
from jax import lax
from jax.experimental import pallas as pl
from jax.experimental.pallas import tpu as pltpu
from jax.sharding import PartitionSpec as P

ridge = 0.05
wire = jnp.float16
HI = lax.Precision.HIGHEST
f32, bf16 = jnp.float32, jnp.bfloat16

PI_A, PI_B, PI_C = 3.140625, 9.67502593994140625e-4, 1.509957990978376432e-7
SIN = (0.9999999956905781, -0.16666657923140904, 0.008333049389622973, -0.000198089486478871, 2.604931690728071e-06)
VMEM = 50 * 1024 * 1024


def cosine(x):
    whole = jnp.floor(x * (1.0 / math.pi))
    shift = whole + 0.5
    r = ((x - shift * PI_A) - shift * PI_B) - shift * PI_C
    u = r * r
    p = SIN[4]
    for c in SIN[3::-1]:
        p = p * u + c
    s = r * p
    odd = (whole.astype(jnp.int32) & 1) == 1
    return jnp.where(odd, s, -s)


def features_kernel(scale, x_ref, w_ref, p_ref, o_ref):
    pre = jnp.dot(x_ref[...], w_ref[0], preferred_element_type=f32) + p_ref[0].astype(f32)
    o_ref[0] = (cosine(pre) * scale).astype(bf16)


def features(x, w, p, scale):
    rows, depth = x.shape
    blocks, _, width = w.shape
    tile = min(rows, 256)
    return pl.pallas_call(
        functools.partial(features_kernel, scale),
        grid=(blocks, rows // tile),
        in_specs=[
            pl.BlockSpec((tile, depth), lambda b, i: (i, 0)),
            pl.BlockSpec((1, depth, width), lambda b, i: (b, 0, 0)),
            pl.BlockSpec((1, 1, width), lambda b, i: (b, 0, 0)),
        ],
        out_specs=pl.BlockSpec((1, tile, width), lambda b, i: (b, i, 0)),
        out_shape=jax.ShapeDtypeStruct((blocks, rows, width), bf16),
        compiler_params=pltpu.CompilerParams(vmem_limit_bytes=VMEM),
        name="features",
    )(x, w, p.reshape(blocks, 1, width))


def split(a):
    hi = a.astype(bf16)
    return hi, (a - hi.astype(f32)).astype(bf16)


def dot1(a, b):
    return jnp.dot(a, b, preferred_element_type=f32)


def dot3(a, b):
    ah, al = split(a)
    bh, bl = split(b)
    return dot1(ah, bh) + (dot1(ah, bl) + dot1(al, bh))


def dot6(a, b):
    return jnp.dot(a, b, precision=HI, preferred_element_type=f32)


def tdot6(a, b):
    return lax.dot_general(a, b, (((0,), (0,)), ((), ())), precision=HI, preferred_element_type=f32)


def eye(n):
    return (lax.broadcasted_iota(jnp.int32, (n, n), 0) == lax.broadcasted_iota(jnp.int32, (n, n), 1)).astype(f32)


def invert(a_refs, x_refs):
    n = a_refs[0].shape[-1]
    top = jnp.float32(0.0)
    for a in a_refs:
        top = jnp.maximum(top, jnp.max(jnp.sum(jnp.abs(a[...]), axis=1)))
    top = top * 1.0001
    ident = eye(n)
    for x in x_refs:
        x[...] = ident * (1.0 / top)

    def step(low):
        scale = 2.0 / (1.0 + low)
        for a, x in zip(a_refs, x_refs):
            xv = x[...] * scale
            y = dot3(a[...], xv)
            x[...] = 2.0 * xv - dot3(xv, y)
        return jnp.minimum(4.0 * low / ((1.0 + low) * (1.0 + low)) * 0.999, 1.0)

    lax.while_loop(lambda low: low < 0.98, step, 0.9 * ridge / top)
    for a, x in zip(a_refs, x_refs):
        xv = x[...]
        x[...] = 2.0 * xv - dot6(xv, dot6(a[...], xv))


def factor_kernel(inv_n, g_ref, s_ref, o_ref, a_ref, t_ref, v_ref, x_ref, y_ref):
    blocks, width, _ = g_ref.shape
    h = width // 2
    every = range(blocks)
    for b in every:
        s = s_ref[b]
        full = g_ref[b] + tdot6(s, s) * inv_n + ridge * eye(width)
        a_ref[b] = full[:h, :h]
        t_ref[b] = full[h:, :h]
        v_ref[b] = full[h:, h:]
    invert([a_ref.at[b] for b in every], [x_ref.at[b] for b in every])
    for b in every:
        t = t_ref[b]
        v = dot6(t, x_ref[b])
        t_ref[b] = v
        a_ref[b] = v_ref[b] - lax.dot_general(v, t, (((1,), (1,)), ((), ())), precision=HI, preferred_element_type=f32)
    invert([a_ref.at[b] for b in every], [y_ref.at[b] for b in every])
    for b in every:
        v, y = t_ref[b], y_ref[b]
        low = dot6(y, v)
        o_ref[b, h:, h:] = y
        o_ref[b, h:, :h] = -low
        o_ref[b, :h, h:] = -low.T
        o_ref[b, :h, :h] = x_ref[b] + tdot6(v, low)


def factor(g, s, n):
    blocks, width, _ = g.shape
    h = width // 2
    half = pltpu.VMEM((blocks, h, h), f32)
    return pl.pallas_call(
        functools.partial(factor_kernel, 1.0 / n),
        out_shape=jax.ShapeDtypeStruct(g.shape, f32),
        scratch_shapes=[half] * 5,
        compiler_params=pltpu.CompilerParams(vmem_limit_bytes=VMEM),
        name="factor",
    )(g, s)


def solve_kernel(inv_n, pairs, w_ref, x_ref, s_ref, t_ref, c_ref, o_ref, d_ref):
    blocks = w_ref.shape[0]
    ts = t_ref[...]
    deltas = []
    for b in range(blocks):
        rhs = c_ref[b] + tdot6(s_ref[b], ts) * inv_n
        for c in range(b):
            index, flip = pairs[(b, c)]
            dims = (((0,), (0,)), ((), ())) if flip else (((1,), (0,)), ((), ()))
            hi, lo = split(x_ref[index])
            rhs = rhs - (
                lax.dot_general(hi, deltas[c], dims, preferred_element_type=f32)
                + lax.dot_general(lo, deltas[c], dims, preferred_element_type=f32)
            )
        delta = dot6(w_ref[b], rhs)
        rounded = delta.astype(bf16)
        o_ref[b] = delta
        d_ref[b] = rounded
        deltas.append(rounded)
        s = s_ref[b]
        sh, sl = split(s)
        sm = (s - sh.astype(f32) - sl.astype(f32)).astype(bf16)
        ts = ts - (dot1(sh, rounded) + (dot1(sl, rounded) + dot1(sm, rounded)))


def solve(w, x, s, t, c, n, pairs):
    blocks, width, targets = c.shape
    parts = s.shape[1]
    tile = min(targets, 256)
    return pl.pallas_call(
        functools.partial(solve_kernel, 1.0 / n, pairs),
        grid=(targets // tile,),
        in_specs=[
            pl.BlockSpec(w.shape, lambda i: (0, 0, 0)),
            pl.BlockSpec(x.shape, lambda i: (0, 0, 0)),
            pl.BlockSpec(s.shape, lambda i: (0, 0, 0)),
            pl.BlockSpec((parts, tile), lambda i: (0, i)),
            pl.BlockSpec((blocks, width, tile), lambda i: (0, 0, i)),
        ],
        out_specs=[
            pl.BlockSpec((blocks, width, tile), lambda i: (0, 0, i)),
            pl.BlockSpec((blocks, width, tile), lambda i: (0, 0, i)),
        ],
        out_shape=[jax.ShapeDtypeStruct(c.shape, f32), jax.ShapeDtypeStruct(c.shape, bf16)],
        compiler_params=pltpu.CompilerParams(vmem_limit_bytes=VMEM),
        name="solve",
    )(w, x, s, t, c)


def fit_kernel(f_ref, d_ref, t_ref, o_ref):
    total = t_ref[...].astype(f32)
    for b in range(f_ref.shape[0]):
        total = total - dot1(f_ref[b], d_ref[b])
    o_ref[...] = total


def fit(feats, delta, targets):
    blocks, rows, width = feats.shape
    columns = targets.shape[1]
    tile = min(rows, 256)
    return pl.pallas_call(
        fit_kernel,
        grid=(rows // tile,),
        in_specs=[
            pl.BlockSpec((blocks, tile, width), lambda i: (0, i, 0)),
            pl.BlockSpec(delta.shape, lambda i: (0, 0, 0)),
            pl.BlockSpec((tile, columns), lambda i: (i, 0)),
        ],
        out_specs=pl.BlockSpec((tile, columns), lambda i: (i, 0)),
        out_shape=jax.ShapeDtypeStruct((rows, columns), f32),
        compiler_params=pltpu.CompilerParams(vmem_limit_bytes=VMEM),
        name="fit",
    )(feats, delta, targets)


def flip_pairs(bit):
    return [(i, i ^ (1 << bit)) for i in range(lax.axis_size("rows"))]


def reduce_scatter(x, order, scale):
    me = lax.axis_index("rows")
    for bit in order:
        mine = (me >> bit) & 1
        half = x.shape[0] // 2
        send = lax.dynamic_slice_in_dim(x, (1 - mine) * half, half)
        keep = lax.dynamic_slice_in_dim(x, mine * half, half)
        got = lax.ppermute((send * scale).astype(wire), "rows", flip_pairs(bit))
        x = keep + got.astype(f32) * (1.0 / scale)
    return x


def all_gather(x, order):
    me = lax.axis_index("rows")
    for bit in order[::-1]:
        mine = (me >> bit) & 1
        got = lax.ppermute(x, "rows", flip_pairs(bit))
        x = jnp.where(mine == 1, jnp.concatenate([got, x]), jnp.concatenate([x, got]))
    return x


def swap(x):
    cores = lax.axis_size("blk")
    return lax.ppermute(x, "blk", [(i, (i + 1) % cores) for i in range(cores)])


def tdot(a, b):
    return lax.dot_general(a, b, (((0,), (0,)), ((), ())), preferred_element_type=f32)


def body(inputs, proj, phase, targets):
    parts = lax.axis_size("rows")
    core = lax.axis_index("blk")
    n = inputs.shape[0]
    columns = targets.shape[1]
    owned, _, width = proj.shape
    scale = 1.0 / math.sqrt(n * parts)
    gscale = 2.0**15
    cscale = 2.0 ** math.floor(math.log2(65504.0 / (8.0 * math.sqrt(n * parts))))
    bits = list(range(parts.bit_length() - 1))
    order_a = bits
    order_b = [1, 2, 0] + bits[3:]
    order_c = [2, 0, 1] + bits[3:]

    proj2, phase2 = swap(proj), swap(phase)
    own = features(inputs, proj, phase, scale)
    own_sum = jnp.sum(own.astype(f32), axis=1)
    rank1 = lambda a, b: a[:, None] * (b * (1.0 / n))[None, :]
    diag = jnp.concatenate([tdot(own[i], own[i]) - rank1(own_sum[i], own_sum[i]) for i in range(owned)])
    diag = reduce_scatter(diag, order_a, gscale)

    other = features(inputs, proj2, phase2, scale)
    other_sum = jnp.sum(other.astype(f32), axis=1)
    tsum = jnp.sum(targets.astype(f32), axis=0)
    feats = jnp.concatenate([own, other])
    sums = jnp.concatenate([own_sum, other_sum])
    corr = jnp.concatenate([tdot(feats[i], targets) - rank1(sums[i], tsum) for i in range(2 * owned)])
    corr = reduce_scatter(corr, order_b, cscale)
    left = [own[1], other[core], other[1 - core]]
    left_sum = [own_sum[1], other_sum[core], other_sum[1 - core]]
    right = [own[0], own[0], own[1]]
    right_sum = [own_sum[0], own_sum[0], own_sum[1]]
    cross = jnp.concatenate([tdot(a, b) - rank1(p, q) for a, b, p, q in zip(left, right, left_sum, right_sum)])
    cross = reduce_scatter(cross, order_c, gscale)

    extra = jnp.concatenate([sums, tsum.reshape(-1, width)])
    high = extra.astype(wire)
    low = (extra - high.astype(f32)).astype(wire)
    extra = jnp.concatenate([high, low])
    extra = jnp.pad(extra, ((0, -extra.shape[0] % 16), (0, 0)))
    piece = diag.shape[0]
    got = all_gather(jnp.concatenate([(diag * gscale).astype(wire), extra]), order_a).reshape(parts, -1, width)
    gram = got[:, :piece].reshape(owned, width, width).astype(f32) * (1.0 / gscale)
    count = 2 * owned + columns // width
    extra = got[:, piece : piece + count].astype(f32) + got[:, piece + count : piece + 2 * count].astype(f32)
    sums = extra[:, : 2 * owned].transpose(1, 0, 2)
    tsums = extra[:, 2 * owned :].reshape(parts, columns)
    mine = factor(gram, sums[:owned], n)

    corr = all_gather((corr * cscale).astype(wire), order_b).reshape(2 * owned, width, columns).astype(f32) * (1.0 / cscale)
    cross = all_gather((cross * gscale).astype(wire), order_c)
    cross2 = swap(cross)
    theirs = swap(mine)
    first = core == 0
    both = lambda a, b: jnp.concatenate([jnp.where(first, a, b), jnp.where(first, b, a)])
    cross = both(cross, cross2).astype(f32).reshape(-1, width, width) * (1.0 / gscale)
    inverse = both(mine, theirs)
    sums = both(sums[:owned], sums[owned:])
    corr = both(corr[:owned], corr[owned:])
    pairs = {(1, 0): (0, False), (2, 0): (1, False), (3, 1): (2, False), (3, 2): (3, False), (2, 1): (4, True), (3, 0): (5, True)}
    coefs, delta = solve(inverse, cross, sums, tsums, corr, n, pairs)
    delta = jnp.where(first, delta, jnp.concatenate([delta[owned:], delta[:owned]]))
    residual = fit(feats, delta, targets)
    return (coefs, residual)


def solution(mesh):
    return jax.shard_map(
        body,
        mesh=mesh,
        in_specs=(P("rows", None), P("blk", None, None), P("blk", None), P("rows", "blk")),
        out_specs=(P(None, None, "blk"), P("rows", "blk")),
        check_vma=False,
    )
```

```python
import functools
import math

import jax
import jax.numpy as jnp
from jax import lax
from jax.experimental import pallas as pl
from jax.experimental.pallas import tpu as pltpu
from jax.sharding import PartitionSpec as P

ridge = 0.05
wire = jnp.float16
HI = lax.Precision.HIGHEST
f32, bf16 = jnp.float32, jnp.bfloat16

SIN = (6.283185280262748, -41.341680654656756, 81.60247856840721, -76.58120078779972, 39.75982743860689)
MIB = 1024 * 1024


def cosine(x, scale):
    turns = x * (0.5 / math.pi)
    w = 0.25 - jnp.abs(turns - jnp.round(turns))
    u = w * w
    p = SIN[4] * scale
    for c in SIN[3::-1]:
        p = p * u + c * scale
    return w * p


def features(scale, x_ref, w_ref, p_ref, f_ref, s_ref):
    rows = x_ref.shape[0]
    tile = min(rows, 256)
    for b in range(w_ref.shape[0]):
        total = 0.0
        for i in range(rows // tile):
            at = pl.ds(i * tile, tile)
            pre = dot1(x_ref[at], w_ref[b]) + p_ref[b].astype(f32)
            out = cosine(pre, scale).astype(bf16)
            f_ref[b, at] = out
            total = total + jnp.sum(out.astype(f32), axis=0, keepdims=True)
        s_ref[b] = total


def tdot(a, b):
    return lax.dot_general(a, b, (((0,), (0,)), ((), ())), preferred_element_type=f32)


def outer(a, b):
    return jnp.broadcast_to(a, (128, a.shape[1])).T[:, :1] * b


def own_kernel(scale, x_ref, w_ref, p_ref, t_ref, f_ref, s_ref, ts_ref, g_ref, d_ref, c_ref):
    rows = x_ref.shape[0]
    blocks, _, width = w_ref.shape
    h = width // 2
    features(scale, x_ref, w_ref, p_ref, f_ref, s_ref)
    ts = jnp.sum(t_ref[...].astype(f32), axis=0, keepdims=True)
    ts_ref[...] = ts
    row = lax.broadcasted_iota(jnp.int32, (h, h), 0)
    col = lax.broadcasted_iota(jnp.int32, (h, h), 1)
    for b in range(blocks):
        low, high = f_ref[b, :, :h], f_ref[b, :, h:]
        turned = f_ref[b].T
        s = s_ref[b]
        back = outer(s, s) * (1.0 / rows)
        corner = dot1(turned[h:], high) - back[h:, h:]
        at = pl.ds(b * h, h)
        g_ref[at, h:] = jnp.where(row >= col, dot1(turned[:h], low) - back[:h, :h], corner)
        g_ref[at, :h] = dot1(turned[h:], low) - back[h:, :h]
        d_ref[b] = jnp.sum(jnp.where(row == col, corner, 0.0), axis=0, keepdims=True)
        c_ref[pl.ds(b * width, width)] = dot1(turned, t_ref[...]) - outer(s, ts) * (1.0 / rows)


def other_kernel(scale, core_ref, x_ref, w_ref, p_ref, t_ref, ts_ref, f_ref, s_ref, f2_ref, s2_ref, c_ref, x2_ref):
    rows = x_ref.shape[0]
    blocks, _, width = w_ref.shape
    features(scale, x_ref, w_ref, p_ref, f2_ref, s2_ref)
    for b in range(blocks):
        c_ref[pl.ds(b * width, width)] = tdot(f2_ref[b], t_ref[...]) - outer(s2_ref[b], ts_ref[...]) * (1.0 / rows)
    core = core_ref[0]
    made = ((f_ref, s_ref, 1, 0), (f2_ref, s2_ref, core, 0), (f2_ref, s2_ref, 1 - core, 1))
    for i, (feats, sums, left, right) in enumerate(made):
        product = tdot(feats[left], f_ref[right]) - outer(sums[left], s_ref[right]) * (1.0 / rows)
        x2_ref[pl.ds(i * width, width)] = product


def split(a):
    hi = a.astype(bf16)
    return hi, (a - hi.astype(f32)).astype(bf16)


def dot1(a, b):
    return jnp.dot(a, b, preferred_element_type=f32)


def dot3(a, b):
    ah, al = split(a)
    bh, bl = split(b)
    return dot1(ah, bh) + (dot1(ah, bl) + dot1(al, bh))


def dot6(a, b):
    return jnp.dot(a, b, precision=HI, preferred_element_type=f32)


def tdot6(a, b):
    return lax.dot_general(a, b, (((0,), (0,)), ((), ())), precision=HI, preferred_element_type=f32)


def thirds(a):
    hi, lo = split(a)
    return hi, lo, (a - hi.astype(f32) - lo.astype(f32)).astype(bf16)


def narrow(a, b):
    ah, am, al = thirds(a)
    bh, bm, bl = thirds(b)
    left = jnp.concatenate([al, ah, am, am, ah, ah])
    return lax.dot_general(left, jnp.concatenate([bh, bl, bm, bh, bm, bh]), (((0,), (0,)), ((), ())), preferred_element_type=f32)


def eye(n):
    return (lax.broadcasted_iota(jnp.int32, (n, n), 0) == lax.broadcasted_iota(jnp.int32, (n, n), 1)).astype(f32)


def invert(a_refs, x_refs):
    n = a_refs[0].shape[-1]
    top = jnp.float32(0.0)
    for a in a_refs:
        top = jnp.maximum(top, jnp.max(jnp.sum(jnp.abs(a[...]), axis=1)))
    top = top * 1.0001
    ident = eye(n)
    for x in x_refs:
        x[...] = ident * (1.0 / top)

    def step(low):
        scale = 2.0 / (1.0 + low)
        for a, x in zip(a_refs, x_refs):
            xv = x[...] * scale
            y = dot3(a[...], xv)
            x[...] = 2.0 * xv - dot3(xv, y)
        return jnp.minimum(4.0 * low / ((1.0 + low) * (1.0 + low)) * 0.999, 1.0)

    lax.while_loop(lambda low: low < 0.98, step, 0.9 * ridge / top)
    for a, x in zip(a_refs, x_refs):
        xv = x[...]
        x[...] = 2.0 * xv - dot6(xv, dot6(a[...], xv))


def cost(us):
    return pl.CostEstimate(flops=int(us * 1.15e9), bytes_accessed=0, transcendentals=0)


def call(kernel, us, out_shape, *args):
    return pl.pallas_call(
        kernel,
        in_specs=[pl.BlockSpec(memory_space=pltpu.SMEM) if a.dtype == jnp.int32 else pl.BlockSpec(a.shape) for a in args],
        out_shape=out_shape,
        cost_estimate=cost(us),
        compiler_params=pltpu.CompilerParams(vmem_limit_bytes=24 * MIB),
        name=kernel.func.__name__ if isinstance(kernel, functools.partial) else kernel.__name__,
    )(*args)


def head_kernel(inv_n, g_ref, d_ref, s_ref, a_ref, t_ref, v_ref, x_ref):
    blocks, h, _ = g_ref.shape
    row = lax.broadcasted_iota(jnp.int32, (h, h), 0)
    col = lax.broadcasted_iota(jnp.int32, (h, h), 1)
    for b in range(blocks):
        s = s_ref[b]
        back = narrow(s, s) * inv_n
        both = g_ref[b, :, h:]
        turned = both.T
        ident = jnp.where(row == col, ridge, 0.0)
        a_ref[b] = jnp.where(row >= col, both, turned) + back[:h, :h] + ident
        t_ref[b] = g_ref[b, :, :h] + back[h:, :h]
        v_ref[b] = jnp.where(row < col, both, jnp.where(row == col, d_ref[b], turned)) + back[h:, h:] + ident
    invert([a_ref.at[b] for b in range(blocks)], [x_ref.at[b] for b in range(blocks)])


def tail_kernel(t_ref, v_ref, x_ref, a_ref, y_ref, o_ref):
    blocks, h, _ = t_ref.shape
    every = range(blocks)
    turns = []
    for b in every:
        t = t_ref[b]
        v = dot6(t, x_ref[b])
        turns.append(v)
        a_ref[b] = v_ref[b] - lax.dot_general(v, t, (((1,), (1,)), ((), ())), precision=HI, preferred_element_type=f32)
    invert([a_ref.at[b] for b in every], [y_ref.at[b] for b in every])
    for b in every:
        v, y = turns[b], y_ref[b]
        low = dot6(y, v)
        o_ref[b, h:, h:] = y
        o_ref[b, h:, :h] = -low
        o_ref[b, :h, h:] = -low.T
        o_ref[b, :h, :h] = x_ref[b] + tdot6(v, low)


def head(g, d, s, n):
    shape = jax.ShapeDtypeStruct((g.shape[0], g.shape[1], g.shape[1]), f32)
    _, t, v, x = call(functools.partial(head_kernel, 1.0 / n), 10, [shape] * 4, g, d, s)
    return t, v, x


def tail(t, v, x):
    blocks, h, _ = t.shape
    half = jax.ShapeDtypeStruct(t.shape, f32)
    return call(tail_kernel, 10, [half, half, jax.ShapeDtypeStruct((blocks, 2 * h, 2 * h), f32)], t, v, x)[2]


def pick(first, owner, own, other):
    return jnp.where(first, own, other) if owner == 0 else jnp.where(first, other, own)


def solve_kernel(inv_n, owned, core_ref, w_ref, w2_ref, x_ref, x2_ref, s_ref, s2_ref, t_ref, c_ref, c2_ref, f_ref, f2_ref, y_ref, o_ref, r_ref, d_ref, ts_ref, xv_ref, xv2_ref, sem):
    first = core_ref[0] == 0
    step = pl.program_id(0)
    copies = [pltpu.make_async_copy(x_ref, xv_ref, sem.at[0]), pltpu.make_async_copy(x2_ref, xv2_ref, sem.at[1])]

    def block(b):
        owner, local = b // owned, b % owned
        if b == 0:
            for copy in copies:
                copy.start()
            ts_ref[...] = t_ref[...]
            r_ref[...] = y_ref[...].astype(f32)
        if b == 1:
            for copy in copies:
                copy.wait()
        s = pick(first, owner, s_ref[local], s2_ref[local])
        ts = ts_ref[...]
        rhs = pick(first, owner, c_ref[0], c2_ref[0]) + narrow(s, ts) * inv_n
        for c in range(b):
            index, keeper = PAIRS[(b, c)]
            dims = (((0,), (0,)), ((), ())) if (keeper == 1 and index > 0) else (((1,), (0,)), ((), ()))
            hi, lo = split(pick(first, keeper, xv_ref[index], xv2_ref[index]))
            rhs = rhs - (
                lax.dot_general(hi, d_ref[c], dims, preferred_element_type=f32)
                + lax.dot_general(lo, d_ref[c], dims, preferred_element_type=f32)
            )
        delta = dot3(pick(first, owner, w_ref[0], w2_ref[0]), rhs)
        rounded = delta.astype(bf16)
        o_ref[0] = delta
        d_ref[b] = rounded
        sh, sl, sm = thirds(s)
        ts_ref[...] = ts - (dot1(sh, rounded) + (dot1(sl, rounded) + dot1(sm, rounded)))
        r_ref[...] -= dot1(pick(first, owner, f_ref[0], f2_ref[0]), rounded)

    for b in range(2 * owned):
        pl.when(step == b)(functools.partial(block, b))


def solve(core, w, w2, x, x2, s, s2, t, c, c2, f, f2, y, n):
    owned, width, columns = c.shape
    blocks = 2 * owned
    rows = f.shape[1]
    whole = lambda a: pl.BlockSpec(a.shape, lambda b: (0,) * a.ndim)
    local = lambda a: pl.BlockSpec((1,) + a.shape[1:], lambda b: (b % owned, 0, 0))
    anywhere = pl.BlockSpec(memory_space=pl.ANY)
    return pl.pallas_call(
        functools.partial(solve_kernel, 1.0 / n, owned),
        grid=(blocks,),
        in_specs=[pl.BlockSpec(memory_space=pltpu.SMEM), local(w), local(w2), anywhere, anywhere, whole(s), whole(s2)]
        + [whole(t), local(c), local(c2), local(f), local(f2), whole(y)],
        out_specs=[
            pl.BlockSpec((1, width, columns), lambda b: (b, 0, 0)),
            pl.BlockSpec((rows, columns), lambda b: (0, 0)),
        ],
        out_shape=[jax.ShapeDtypeStruct((blocks, width, columns), f32), jax.ShapeDtypeStruct((rows, columns), f32)],
        scratch_shapes=[
            pltpu.VMEM((blocks, width, columns), bf16),
            pltpu.VMEM(t.shape, f32),
            pltpu.VMEM(x.shape, f32),
            pltpu.VMEM(x2.shape, f32),
            pltpu.SemaphoreType.DMA((2,)),
        ],
        compiler_params=pltpu.CompilerParams(vmem_limit_bytes=40 * MIB),
        cost_estimate=cost(15),
        name="solve",
    )(core.reshape(1), w, w2, x, x2, s, s2, t, c, c2, f, f2, y)


PAIRS = {(1, 0): (0, 0), (2, 0): (1, 0), (3, 1): (2, 0), (3, 2): (0, 1), (2, 1): (1, 1), (3, 0): (2, 1)}


def tie(x, after):
    if after is None:
        return x
    return x + (after[(slice(0, 1),) * after.ndim].reshape((1,) * x.ndim).astype(f32) * 0.0).astype(x.dtype)


ORDERS = ((0, 2, 1), (1, 2, 0), (0, 1, 2), (2, 0, 1))


class Chain:
    def __init__(self, x, order, scale):
        self.x, self.order, self.scale = x, order, scale
        self.step = 0
        self.extra = None

    def run(self, after=None):
        count = len(self.order)
        halving = self.step < count
        bit = self.order[self.step if halving else 2 * count - 1 - self.step]
        mine = (lax.axis_index("rows") >> bit) & 1
        pairs = [(i, i ^ (1 << bit)) for i in range(lax.axis_size("rows"))]
        if halving:
            half = self.x.shape[0] // 2
            send = lax.dynamic_slice_in_dim(self.x, (1 - mine) * half, half)
            keep = lax.dynamic_slice_in_dim(self.x, mine * half, half)
            self.sent = tie(send * self.scale, after).astype(wire)
            got = lax.ppermute(self.sent, "rows", pairs)
            self.x = keep + got.astype(f32) * (1.0 / self.scale)
        else:
            if self.step == count:
                self.x = (self.x * self.scale).astype(wire)
                if self.extra is not None:
                    self.x = jnp.concatenate([self.x, self.extra])
            x = tie(self.x, after)
            got = lax.ppermute(x, "rows", pairs)
            self.x = jnp.where(mine == 1, jnp.concatenate([got, x]), jnp.concatenate([x, got]))
        self.step += 1

    def done(self):
        return self.step == 2 * len(self.order)


def swap(x):
    cores = lax.axis_size("blk")
    return lax.ppermute(x, "blk", [(i, (i + 1) % cores) for i in range(cores)])


def body(inputs, proj, phase, targets):
    parts = lax.axis_size("rows")
    core = lax.axis_index("blk")
    n = inputs.shape[0]
    columns = targets.shape[1]
    owned, _, width = proj.shape
    h = width // 2
    scale = 1.0 / math.sqrt(n * parts)
    gscale = 2.0**15
    cscale = 2.0 ** math.floor(math.log2(65504.0 / (8.0 * math.sqrt(n * parts))))
    bits = list(range(parts.bit_length() - 1))
    order_a, order_b, order_c, order_d = ([order[i] for i in range(min(3, len(bits)))] + bits[3:] for order in ORDERS)

    proj2, phase2 = swap(proj), swap(phase)
    shape = lambda *dims: jax.ShapeDtypeStruct(dims, f32)
    feats = jax.ShapeDtypeStruct((owned, n, width), bf16)
    own, own_sum, tsum, packed, corner, c = call(
        functools.partial(own_kernel, scale),
        10,
        [feats, shape(owned, 1, width), shape(1, columns), shape(owned * h, width), shape(owned, 1, h), shape(owned * width, columns)],
        inputs, proj, phase[:, None], targets,
    )
    gram = Chain(packed, order_a, gscale)
    gram.run()
    corr1 = Chain(c, order_b, cscale)
    corr1.run()
    extra = jnp.concatenate([own_sum[:, 0], corner.reshape(-1, width) * gscale, tsum.reshape(-1, width)])
    high = extra.astype(wire)
    gram.extra = jnp.concatenate([high, (extra - high.astype(f32)).astype(wire)])

    other, other_sum, c2, cross = call(
        functools.partial(other_kernel, scale),
        10,
        [feats, shape(owned, 1, width), shape(owned * width, columns), shape(3 * width, width)],
        core.reshape(1), inputs, proj2, phase2[:, None], targets, tsum, own, own_sum,
    )
    corr2 = Chain(c2, order_c, cscale)
    cross = Chain(cross, order_d, gscale)
    gram.run(other_sum)
    corr2.run()
    cross.run()
    while not gram.done():
        gram.run()

    piece = packed.shape[0] // parts
    count = gram.extra.shape[0] // 2
    got = gram.x.reshape(parts, -1, width)
    extra = got[:, piece : piece + count].astype(f32) + got[:, piece + count :].astype(f32)
    g = got[:, :piece].reshape(owned, h, width).astype(f32) * (1.0 / gscale)
    s = extra[:, :owned].transpose(1, 0, 2)
    d = jnp.sum(extra[:, owned : owned + owned * h // width], axis=0).reshape(owned, 1, h) * (1.0 / gscale)
    ts = extra[:, owned + owned * h // width :].reshape(parts, columns)
    s2 = swap(s)
    t, v, x = head(g, d, s, n)
    w = tail(t, v, x)
    w2 = swap(w)

    steps = 2 * len(bits)
    for chain in (corr1, corr2, cross):
        while not chain.done():
            left = steps - chain.step
            chain.run(x if left == 3 else w if left == 2 else None)
    x2 = swap(cross.x)
    wide = lambda a, by: a.reshape(-1, width, a.shape[-1]).astype(f32) * (1.0 / by)
    c, c2 = wide(corr1.x, cscale), wide(corr2.x, cscale)
    return tuple(solve(core, w, w2, wide(cross.x, gscale), wide(x2, gscale), s, s2, ts, c, c2, own, other, targets, n))


def solution(mesh):
    return jax.shard_map(
        body,
        mesh=mesh,
        in_specs=(P("rows", None), P("blk", None, None), P("blk", None), P("rows", "blk")),
        out_specs=(P(None, None, "blk"), P("rows", "blk")),
        check_vma=False,
    )
```

```python
import functools
import math

import jax
import jax.numpy as jnp
from jax import lax
from jax.experimental import pallas as pl
from jax.experimental.pallas import tpu as pltpu
from jax.sharding import PartitionSpec as P

ridge = 0.05
wire = jnp.float16
HI = lax.Precision.HIGHEST
f32, bf16 = jnp.float32, jnp.bfloat16

SIN = (6.283185280262748, -41.341680654656756, 81.60247856840721, -76.58120078779972, 39.75982743860689)
MIB = 1024 * 1024


def cosine(x, scale):
    turns = x * (0.5 / math.pi)
    w = 0.25 - jnp.abs(turns - jnp.round(turns))
    u = w * w
    p = SIN[4] * scale
    for c in SIN[3::-1]:
        p = p * u + c * scale
    return w * p


def features(scale, x_ref, w_ref, p_ref, f_ref, s_ref):
    rows = x_ref.shape[0]
    tile = min(rows, 256)
    for b in range(w_ref.shape[0]):
        total = 0.0
        for i in range(rows // tile):
            at = pl.ds(i * tile, tile)
            pre = dot1(x_ref[at], w_ref[b]) + p_ref[pl.ds(b, 1), :].astype(f32)
            out = cosine(pre, scale).astype(bf16)
            f_ref[b, at] = out
            total = total + jnp.sum(out.astype(f32), axis=0, keepdims=True)
        s_ref[b] = total


def tdot(a, b):
    return lax.dot_general(a, b, (((0,), (0,)), ((), ())), preferred_element_type=f32)


def outer(a, b):
    return jnp.broadcast_to(a, (128, a.shape[1])).T[:, :1] * b


def own_products(scale, x_ref, w_ref, p_ref, t_ref, f_ref, s_ref, ts_ref, g_ref, d_ref, c_ref):
    rows = x_ref.shape[0]
    blocks, _, width = w_ref.shape
    h = width // 2
    features(scale, x_ref, w_ref, p_ref, f_ref, s_ref)
    ts = jnp.sum(t_ref[...].astype(f32), axis=0, keepdims=True)
    ts_ref[...] = ts
    row = lax.broadcasted_iota(jnp.int32, (h, h), 0)
    col = lax.broadcasted_iota(jnp.int32, (h, h), 1)
    for b in range(blocks):
        low, high = f_ref[b, :, :h], f_ref[b, :, h:]
        turned = f_ref[b].T
        s = s_ref[b]
        back = outer(s, s) * (1.0 / rows)
        corner = dot1(turned[h:], high) - back[h:, h:]
        at = pl.ds(b * h, h)
        g_ref[at, h:] = jnp.where(row >= col, dot1(turned[:h], low) - back[:h, :h], corner)
        g_ref[at, :h] = dot1(turned[h:], low) - back[h:, :h]
        d_ref[b] = jnp.sum(jnp.where(row == col, corner, 0.0), axis=0, keepdims=True)
        c_ref[pl.ds(b * width, width)] = dot1(turned, t_ref[...]) - outer(s, ts) * (1.0 / rows)


def other_products(scale, core_ref, x_ref, w_ref, p_ref, t_ref, ts_ref, f_ref, s_ref, f2_ref, s2_ref, c_ref, x2_ref):
    rows = x_ref.shape[0]
    blocks, _, width = w_ref.shape
    features(scale, x_ref, w_ref, p_ref, f2_ref, s2_ref)
    for b in range(blocks):
        c_ref[pl.ds(b * width, width)] = tdot(f2_ref[b], t_ref[...]) - outer(s2_ref[b], ts_ref[...]) * (1.0 / rows)
    core = core_ref[0]
    made = ((f_ref, s_ref, 1, 0), (f2_ref, s2_ref, core, 0), (f2_ref, s2_ref, 1 - core, 1))
    for i, (feats, sums, left, right) in enumerate(made):
        product = tdot(feats[left], f_ref[right]) - outer(sums[left], s_ref[right]) * (1.0 / rows)
        x2_ref[pl.ds(i * width, width)] = product


def prelude_kernel(scale, core_ref, x_any, w_any, p_ref, w2_any, p2_ref, t_any, f_ref, s_ref, ts_ref, g_ref, d_ref, c_ref, f2_ref, s2_ref, c2_ref, x2_ref, x_ref, w_ref, w2_ref, t_ref, sem):
    moves = ((x_any, x_ref), (w_any, w_ref), (t_any, t_ref), (w2_any, w2_ref))
    copies = [pltpu.make_async_copy(source, to, sem.at[i]) for i, (source, to) in enumerate(moves)]
    for copy in copies:
        copy.start()
    for copy in copies[:3]:
        copy.wait()
    own_products(scale, x_ref, w_ref, p_ref, t_ref, f_ref, s_ref, ts_ref, g_ref, d_ref, c_ref)
    copies[3].wait()
    other_products(scale, core_ref, x_ref, w2_ref, p2_ref, t_ref, ts_ref, f_ref, s_ref, f2_ref, s2_ref, c2_ref, x2_ref)


def split(a):
    hi = a.astype(bf16)
    return hi, (a - hi.astype(f32)).astype(bf16)


def dot1(a, b):
    return jnp.dot(a, b, preferred_element_type=f32)


def dot3(a, b):
    ah, al = split(a)
    bh, bl = split(b)
    return dot1(ah, bh) + (dot1(ah, bl) + dot1(al, bh))


def dot6(a, b):
    return jnp.dot(a, b, precision=HI, preferred_element_type=f32)


def tdot6(a, b):
    return lax.dot_general(a, b, (((0,), (0,)), ((), ())), precision=HI, preferred_element_type=f32)


def thirds(a):
    hi, lo = split(a)
    return hi, lo, (a - hi.astype(f32) - lo.astype(f32)).astype(bf16)


def narrow(a, b):
    ah, am, al = thirds(a)
    bh, bm, bl = thirds(b)
    left = jnp.concatenate([al, ah, am, am, ah, ah])
    return lax.dot_general(left, jnp.concatenate([bh, bl, bm, bh, bm, bh]), (((0,), (0,)), ((), ())), preferred_element_type=f32)


def eye(n):
    return (lax.broadcasted_iota(jnp.int32, (n, n), 0) == lax.broadcasted_iota(jnp.int32, (n, n), 1)).astype(f32)


def invert(a_refs, x_refs):
    n = a_refs[0].shape[-1]
    top = jnp.float32(0.0)
    for a in a_refs:
        top = jnp.maximum(top, jnp.max(jnp.sum(jnp.abs(a[...]), axis=1)))
    top = top * 1.0001
    ident = eye(n)
    for x in x_refs:
        x[...] = ident * (1.0 / top)

    def step(low):
        scale = 2.0 / (1.0 + low)
        for a, x in zip(a_refs, x_refs):
            xv = x[...] * scale
            y = dot3(a[...], xv)
            x[...] = 2.0 * xv - dot3(xv, y)
        return jnp.minimum(4.0 * low / ((1.0 + low) * (1.0 + low)) * 0.999, 1.0)

    lax.while_loop(lambda low: low < 0.98, step, 0.9 * ridge / top)
    for a, x in zip(a_refs, x_refs):
        xv = x[...]
        x[...] = 2.0 * xv - dot6(xv, dot6(a[...], xv))


def cost(us):
    return pl.CostEstimate(flops=int(us * 1.15e9), bytes_accessed=0, transcendentals=0)


def call(kernel, us, out_shape, *args):
    return pl.pallas_call(
        kernel,
        out_shape=out_shape,
        cost_estimate=cost(us),
        compiler_params=pltpu.CompilerParams(vmem_limit_bytes=32 * MIB),
        name=kernel.func.__name__ if isinstance(kernel, functools.partial) else kernel.__name__,
    )(*args)


def head_kernel(inv_n, g_ref, d_ref, s_ref, a_ref, t_ref, v_ref, x_ref):
    blocks, h, _ = g_ref.shape
    row = lax.broadcasted_iota(jnp.int32, (h, h), 0)
    col = lax.broadcasted_iota(jnp.int32, (h, h), 1)
    for b in range(blocks):
        s = s_ref[b]
        back = narrow(s, s) * inv_n
        both = g_ref[b, :, h:]
        turned = both.T
        ident = jnp.where(row == col, ridge, 0.0)
        a_ref[b] = jnp.where(row >= col, both, turned) + back[:h, :h] + ident
        t_ref[b] = g_ref[b, :, :h] + back[h:, :h]
        v_ref[:, pl.ds(b * h, h)] = jnp.where(row < col, both, jnp.where(row == col, d_ref[b], turned)) + back[h:, h:] + ident
    invert([a_ref.at[b] for b in range(blocks)], [x_ref.at[b] for b in range(blocks)])


def tail_kernel(t_ref, v_ref, x_ref, a_ref, y_ref, o_ref):
    blocks, h, _ = t_ref.shape
    every = range(blocks)
    turns = []
    for b in every:
        t = t_ref[b]
        v = dot6(t, x_ref[b])
        turns.append(v)
        a_ref[b] = v_ref[:, pl.ds(b * h, h)] - lax.dot_general(v, t, (((1,), (1,)), ((), ())), precision=HI, preferred_element_type=f32)
    invert([a_ref.at[b] for b in every], [y_ref.at[b] for b in every])
    for b in every:
        v, y = turns[b], y_ref[b]
        low = dot6(y, v)
        o_ref[b, h:, h:] = y
        o_ref[b, h:, :h] = -low
        o_ref[b, :h, h:] = -low.T
        o_ref[b, :h, :h] = x_ref[b] + tdot6(v, low)


def head(g, d, s, n):
    shape = jax.ShapeDtypeStruct((g.shape[0], g.shape[1], g.shape[1]), f32)
    side = jax.ShapeDtypeStruct((g.shape[1], g.shape[0] * g.shape[1]), f32)
    _, t, v, x = call(functools.partial(head_kernel, 1.0 / n), 10, [shape, shape, side, shape], g, d, s)
    return t, v, x


def tail(t, v, x):
    blocks, h, _ = t.shape
    half = jax.ShapeDtypeStruct(t.shape, f32)
    return call(tail_kernel, 10, [half, half, jax.ShapeDtypeStruct((blocks, 2 * h, 2 * h), f32)], t, v, x)[2]


def pick(first, owner, own, other):
    return jnp.where(first, own, other) if owner == 0 else jnp.where(first, other, own)


def solve_kernel(inv_n, owned, core_ref, w_ref, w2_ref, x_ref, x2_ref, s_ref, s2_ref, t_ref, c_ref, c2_ref, f_ref, f2_ref, y_ref, o_ref, r_ref, d_ref, ts_ref, xv_ref, xv2_ref, sem):
    first = core_ref[0] == 0
    step = pl.program_id(0)
    copies = [pltpu.make_async_copy(x_ref, xv_ref, sem.at[0]), pltpu.make_async_copy(x2_ref, xv2_ref, sem.at[1])]

    def block(b):
        owner, local = b // owned, b % owned
        if b == 0:
            for copy in copies:
                copy.start()
            ts_ref[...] = t_ref[...]
            r_ref[...] = y_ref[...].astype(f32)
        if b == 1:
            for copy in copies:
                copy.wait()
        s = pick(first, owner, s_ref[local], s2_ref[local])
        ts = ts_ref[...]
        rhs = pick(first, owner, c_ref[0], c2_ref[0]) + narrow(s, ts) * inv_n
        for c in range(b):
            index, keeper = PAIRS[(b, c)]
            dims = (((0,), (0,)), ((), ())) if (keeper == 1 and index > 0) else (((1,), (0,)), ((), ()))
            hi, lo = split(pick(first, keeper, xv_ref[index], xv2_ref[index]))
            rhs = rhs - (
                lax.dot_general(hi, d_ref[c], dims, preferred_element_type=f32)
                + lax.dot_general(lo, d_ref[c], dims, preferred_element_type=f32)
            )
        delta = dot3(pick(first, owner, w_ref[0], w2_ref[0]), rhs)
        rounded = delta.astype(bf16)
        o_ref[0] = delta
        d_ref[b] = rounded
        sh, sl, sm = thirds(s)
        ts_ref[...] = ts - (dot1(sh, rounded) + (dot1(sl, rounded) + dot1(sm, rounded)))
        r_ref[...] -= dot1(pick(first, owner, f_ref[0], f2_ref[0]), rounded)

    for b in range(2 * owned):
        pl.when(step == b)(functools.partial(block, b))


def solve(core, w, w2, x, x2, s, s2, t, c, c2, f, f2, y, n):
    owned, width, columns = c.shape
    blocks = 2 * owned
    rows = f.shape[1]
    whole = lambda a: pl.BlockSpec(a.shape, lambda b: (0,) * a.ndim)
    local = lambda a: pl.BlockSpec((1,) + a.shape[1:], lambda b: (b % owned, 0, 0))
    anywhere = pl.BlockSpec(memory_space=pl.ANY)
    return pl.pallas_call(
        functools.partial(solve_kernel, 1.0 / n, owned),
        grid=(blocks,),
        in_specs=[pl.BlockSpec(memory_space=pltpu.SMEM), local(w), local(w2), anywhere, anywhere, whole(s), whole(s2)]
        + [whole(t), local(c), local(c2), local(f), local(f2), whole(y)],
        out_specs=[
            pl.BlockSpec((1, width, columns), lambda b: (b, 0, 0)),
            pl.BlockSpec((rows, columns), lambda b: (0, 0)),
        ],
        out_shape=[jax.ShapeDtypeStruct((blocks, width, columns), f32), jax.ShapeDtypeStruct((rows, columns), f32)],
        scratch_shapes=[
            pltpu.VMEM((blocks, width, columns), bf16),
            pltpu.VMEM(t.shape, f32),
            pltpu.VMEM(x.shape, f32),
            pltpu.VMEM(x2.shape, f32),
            pltpu.SemaphoreType.DMA((2,)),
        ],
        compiler_params=pltpu.CompilerParams(vmem_limit_bytes=40 * MIB),
        cost_estimate=cost(15),
        name="solve",
    )(core.reshape(1), w, w2, x, x2, s, s2, t, c, c2, f, f2, y)


PAIRS = {(1, 0): (0, 0), (2, 0): (1, 0), (3, 1): (2, 0), (3, 2): (0, 1), (2, 1): (1, 1), (3, 0): (2, 1)}


def tie(x, *after):
    for one in after:
        rows = min(x.shape[0], one.shape[0])
        zero = (one[:rows].astype(f32) * 0.0).astype(x.dtype)
        x = x + jnp.pad(zero, ((0, x.shape[0] - rows), (0, 0)))
    return x


ORDERS = ((0, 2, 1), (1, 2, 0), (0, 1, 2), (2, 0, 1))


class Chain:
    def __init__(self, x, order, scale):
        self.x, self.order, self.scale = x, order, scale
        self.step = 0
        self.extra = None

    def run(self, *after):
        count = len(self.order)
        halving = self.step < count
        bit = self.order[self.step if halving else 2 * count - 1 - self.step]
        mine = (lax.axis_index("rows") >> bit) & 1
        pairs = [(i, i ^ (1 << bit)) for i in range(lax.axis_size("rows"))]
        if halving:
            half = self.x.shape[0] // 2
            send = lax.dynamic_slice_in_dim(self.x, (1 - mine) * half, half)
            keep = lax.dynamic_slice_in_dim(self.x, mine * half, half)
            send = tie(send * self.scale, *after).astype(wire)
            self.got = got = lax.ppermute(send, "rows", pairs)
            self.x = keep + got.astype(f32) * (1.0 / self.scale)
        else:
            if self.step == count:
                self.x = (self.x * self.scale).astype(wire)
                if self.extra is not None:
                    self.x = jnp.concatenate([self.x, self.extra])
            x = tie(self.x, *after)
            self.got = got = lax.ppermute(x, "rows", pairs)
            self.x = jnp.where(mine == 1, jnp.concatenate([got, x]), jnp.concatenate([x, got]))
        self.step += 1

    def done(self):
        return self.step == 2 * len(self.order)


def groups(low):
    parts = lax.axis_size("rows")
    near = [[i + j for j in range(low)] for i in range(0, parts, low)]
    far = [[i + j for j in range(0, parts, low)] for i in range(low)]
    return near, far


def scatter_sum(x, scale, cut):
    x = (x * scale).astype(wire).reshape(len(cut[0]), -1, x.shape[-1])
    x = lax.all_to_all(x, "rows", 0, 0, axis_index_groups=cut)
    return jnp.sum(x.astype(f32), axis=0) * (1.0 / scale)


def swap(x):
    cores = lax.axis_size("blk")
    return lax.ppermute(x, "blk", [(i, (i + 1) % cores) for i in range(cores)])


def body(inputs, proj, phase, targets):
    parts = lax.axis_size("rows")
    core = lax.axis_index("blk")
    n = inputs.shape[0]
    columns = targets.shape[1]
    owned, _, width = proj.shape
    h = width // 2
    scale = 1.0 / math.sqrt(n * parts)
    gscale = 2.0**15
    cscale = 2.0 ** math.floor(math.log2(65504.0 / (8.0 * math.sqrt(n * parts))))
    bits = list(range(parts.bit_length() - 1))
    order_a, order_b, order_c, order_d = ([order[i] for i in range(min(3, len(bits)))] + bits[3:] for order in ORDERS)

    proj2, phase2 = swap(proj), swap(phase)
    shape = lambda *dims: jax.ShapeDtypeStruct(dims, f32)
    feats = jax.ShapeDtypeStruct((owned, n, width), bf16)
    sums, corrs = shape(owned, 1, width), shape(owned * width, columns)
    first = [feats, sums, shape(1, columns), shape(owned * h, width), shape(owned, 1, h), corrs]
    place = lambda space: pl.BlockSpec(memory_space=space)
    outs = first + [feats, sums, corrs, shape(3 * width, width)]
    moved = [inputs, proj, proj2, targets]
    own, own_sum, tsum, packed, corner, c, other, other_sum, c2, cross = pl.pallas_call(
        functools.partial(prelude_kernel, scale),
        in_specs=[place(pltpu.SMEM)] + [place(space) for space in (pl.ANY, pl.ANY, pltpu.VMEM, pl.ANY, pltpu.VMEM, pl.ANY)],
        out_specs=[pl.BlockSpec(o.shape) if o.dtype == bf16 else place(pltpu.VMEM) for o in outs],
        out_shape=outs,
        scratch_shapes=[pltpu.VMEM(a.shape, a.dtype) for a in moved] + [pltpu.SemaphoreType.DMA((len(moved),))],
        compiler_params=pltpu.CompilerParams(vmem_limit_bytes=52 * MIB),
        cost_estimate=cost(14),
        name="prelude",
    )(core.reshape(1), inputs, proj, phase, proj2, phase2, targets)
    corr1 = Chain(c, order_b, cscale)
    corr1.run()
    extra = jnp.concatenate([own_sum[:, 0], corner.reshape(-1, width) * gscale, tsum.reshape(-1, width)])
    high = extra.astype(wire)
    extra = jnp.concatenate([high, (extra - high.astype(f32)).astype(wire)])
    near, far = groups(min(4, parts))
    gram = scatter_sum(scatter_sum(packed, gscale, near), gscale, far)

    corr2 = Chain(c2, order_c, cscale)
    cross = Chain(cross, order_d, gscale)
    corr2.run()
    cross.run()
    piece, count = gram.shape[0], extra.shape[0] // 2
    gram = jnp.concatenate([(gram * gscale).astype(wire), extra])
    me = lax.axis_index("rows")
    for bit in bits[2:] + bits[:2]:
        got = lax.ppermute(gram, "rows", [(i, i ^ (1 << bit)) for i in range(parts)])
        gram = jnp.where((me >> bit) & 1 == 1, jnp.concatenate([got, gram]), jnp.concatenate([gram, got]))
    got = gram.reshape(parts, -1, width)
    extra = got[:, piece : piece + count].astype(f32) + got[:, piece + count :].astype(f32)
    g = got[:, :piece].reshape(owned, h, width).astype(f32) * (1.0 / gscale)
    s = extra[:, :owned].transpose(1, 0, 2)
    d = jnp.sum(extra[:, owned : owned + owned * h // width], axis=0).reshape(owned, 1, h) * (1.0 / gscale)
    ts = extra[:, owned + owned * h // width :].reshape(parts, columns)
    s2 = swap(s)
    bulk = (cross, corr1, corr2)
    for chain in bulk[1:]:
        while chain.step < 3:
            chain.run()
    g = tie(g.reshape(-1, width), corr1.got, corr2.got).reshape(g.shape)
    t, v, x = head(g, d, s, n)
    for chain in bulk[1:]:
        while chain.step < 4:
            chain.run()
    w = tail(t, tie(v, corr1.got, corr2.got), x)
    w2 = swap(w)
    half = len(bits)
    for chain in bulk:
        while not chain.done():
            chain.run(*{half + 1: (v,), half + 2: (w.reshape(-1, width),)}.get(chain.step, ()))
    x2 = swap(cross.x)
    wide = lambda a, by: a.reshape(-1, width, a.shape[-1]).astype(f32) * (1.0 / by)
    c, c2 = wide(corr1.x, cscale), wide(corr2.x, cscale)
    return tuple(solve(core, w, w2, wide(cross.x, gscale), wide(x2, gscale), s, s2, ts, c, c2, own, other, targets, n))


def solution(mesh):
    return jax.shard_map(
        body,
        mesh=mesh,
        in_specs=(P("rows", None), P("blk", None, None), P("blk", None), P("rows", "blk")),
        out_specs=(P(None, None, "blk"), P("rows", "blk")),
        check_vma=False,
    )
```

```python
import functools
import math

import jax
import jax.numpy as jnp
from jax import lax
from jax.experimental import pallas as pl
from jax.experimental.pallas import tpu as pltpu
from jax.sharding import PartitionSpec as P

ridge = 0.05
wire = jnp.float16
HI = lax.Precision.HIGHEST
f32, bf16 = jnp.float32, jnp.bfloat16

SIN = (6.283185280262748, -41.341680654656756, 81.60247856840721, -76.58120078779972, 39.75982743860689)
MIB = 1024 * 1024


def cosine(x, scale):
    turns = x * (0.5 / math.pi)
    w = 0.25 - jnp.abs(turns - jnp.round(turns))
    u = w * w
    p = SIN[4] * scale
    for c in SIN[3::-1]:
        p = p * u + c * scale
    return w * p


def features(scale, x_ref, w_ref, p_ref, f_ref, s_ref):
    rows = x_ref.shape[0]
    tile = min(rows, 256)
    for b in range(w_ref.shape[0]):
        total = 0.0
        for i in range(rows // tile):
            at = pl.ds(i * tile, tile)
            pre = dot1(x_ref[at], w_ref[b]) + p_ref[pl.ds(b, 1), :].astype(f32)
            out = cosine(pre, scale).astype(bf16)
            f_ref[b, at] = out
            total = total + jnp.sum(out.astype(f32), axis=0, keepdims=True)
        s_ref[b] = total


def tdot(a, b):
    return lax.dot_general(a, b, (((0,), (0,)), ((), ())), preferred_element_type=f32)


def outer(a, b):
    return jnp.broadcast_to(a, (128, a.shape[1])).T[:, :1] * b


def own_products(scale, x_ref, w_ref, p_ref, t_ref, f_ref, s_ref, ts_ref, g_ref, d_ref, c_ref):
    rows = x_ref.shape[0]
    blocks, _, width = w_ref.shape
    h = width // 2
    features(scale, x_ref, w_ref, p_ref, f_ref, s_ref)
    ts = jnp.sum(t_ref[...].astype(f32), axis=0, keepdims=True)
    ts_ref[...] = ts
    row = lax.broadcasted_iota(jnp.int32, (h, h), 0)
    col = lax.broadcasted_iota(jnp.int32, (h, h), 1)
    for b in range(blocks):
        low, high = f_ref[b, :, :h], f_ref[b, :, h:]
        turned = f_ref[b].T
        s = s_ref[b]
        back = outer(s, s) * (1.0 / rows)
        corner = dot1(turned[h:], high) - back[h:, h:]
        at = pl.ds(b * h, h)
        g_ref[at, h:] = jnp.where(row >= col, dot1(turned[:h], low) - back[:h, :h], corner)
        g_ref[at, :h] = dot1(turned[h:], low) - back[h:, :h]
        d_ref[b] = jnp.sum(jnp.where(row == col, corner, 0.0), axis=0, keepdims=True)
        c_ref[pl.ds(b * width, width)] = dot1(turned, t_ref[...]) - outer(s, ts) * (1.0 / rows)


def other_products(scale, core_ref, x_ref, w_ref, p_ref, t_ref, ts_ref, f_ref, s_ref, f2_ref, s2_ref, c_ref, x2_ref):
    rows = x_ref.shape[0]
    blocks, _, width = w_ref.shape
    features(scale, x_ref, w_ref, p_ref, f2_ref, s2_ref)
    for b in range(blocks):
        c_ref[pl.ds(b * width, width)] = tdot(f2_ref[b], t_ref[...]) - outer(s2_ref[b], ts_ref[...]) * (1.0 / rows)
    core = core_ref[0]
    made = ((f_ref, s_ref, 1, 0), (f2_ref, s2_ref, core, 0), (f2_ref, s2_ref, 1 - core, 1))
    for i, (feats, sums, left, right) in enumerate(made):
        product = tdot(feats[left], f_ref[right]) - outer(sums[left], s_ref[right]) * (1.0 / rows)
        x2_ref[pl.ds(i * width, width)] = product


def prelude_kernel(scale, core_ref, x_any, w_any, p_ref, w2_any, p2_ref, t_any, f_ref, s_ref, ts_ref, g_ref, d_ref, c_ref, f2_ref, s2_ref, c2_ref, x2_ref, x_ref, w_ref, w2_ref, t_ref, sem):
    moves = ((x_any, x_ref), (w_any, w_ref), (t_any, t_ref), (w2_any, w2_ref))
    copies = [pltpu.make_async_copy(source, to, sem.at[i]) for i, (source, to) in enumerate(moves)]
    for copy in copies:
        copy.start()
    for copy in copies[:3]:
        copy.wait()
    own_products(scale, x_ref, w_ref, p_ref, t_ref, f_ref, s_ref, ts_ref, g_ref, d_ref, c_ref)
    copies[3].wait()
    other_products(scale, core_ref, x_ref, w2_ref, p2_ref, t_ref, ts_ref, f_ref, s_ref, f2_ref, s2_ref, c2_ref, x2_ref)


def split(a):
    hi = a.astype(bf16)
    return hi, (a - hi.astype(f32)).astype(bf16)


def dot1(a, b):
    return jnp.dot(a, b, preferred_element_type=f32)


def dot3(a, b):
    ah, al = split(a)
    bh, bl = split(b)
    return dot1(ah, bh) + (dot1(ah, bl) + dot1(al, bh))


def dot6(a, b):
    return jnp.dot(a, b, precision=HI, preferred_element_type=f32)


def tdot6(a, b):
    return lax.dot_general(a, b, (((0,), (0,)), ((), ())), precision=HI, preferred_element_type=f32)


def thirds(a):
    hi, lo = split(a)
    return hi, lo, (a - hi.astype(f32) - lo.astype(f32)).astype(bf16)


def narrow(a, b):
    ah, am, al = thirds(a)
    bh, bm, bl = thirds(b)
    left = jnp.concatenate([al, ah, am, am, ah, ah])
    return lax.dot_general(left, jnp.concatenate([bh, bl, bm, bh, bm, bh]), (((0,), (0,)), ((), ())), preferred_element_type=f32)


def eye(n):
    return (lax.broadcasted_iota(jnp.int32, (n, n), 0) == lax.broadcasted_iota(jnp.int32, (n, n), 1)).astype(f32)


def invert(a_refs, x_refs):
    n = a_refs[0].shape[-1]
    top = jnp.float32(0.0)
    for a in a_refs:
        top = jnp.maximum(top, jnp.max(jnp.sum(jnp.abs(a[...]), axis=1)))
    top = top * 1.0001
    ident = eye(n)
    for x in x_refs:
        x[...] = ident * (1.0 / top)

    def step(low):
        scale = 2.0 / (1.0 + low)
        for a, x in zip(a_refs, x_refs):
            xv = x[...] * scale
            y = dot3(a[...], xv)
            x[...] = 2.0 * xv - dot3(xv, y)
        return jnp.minimum(4.0 * low / ((1.0 + low) * (1.0 + low)) * 0.999, 1.0)

    lax.while_loop(lambda low: low < 0.98, step, 0.9 * ridge / top)
    for a, x in zip(a_refs, x_refs):
        xv = x[...]
        x[...] = 2.0 * xv - dot6(xv, dot6(a[...], xv))


def cost(us):
    return pl.CostEstimate(flops=int(us * 1.15e9), bytes_accessed=0, transcendentals=0)


def call(kernel, us, out_shape, *args):
    return pl.pallas_call(
        kernel,
        out_shape=out_shape,
        cost_estimate=cost(us),
        compiler_params=pltpu.CompilerParams(vmem_limit_bytes=32 * MIB),
        name=kernel.func.__name__ if isinstance(kernel, functools.partial) else kernel.__name__,
    )(*args)


def head_kernel(inv_n, g_ref, d_ref, s_ref, a_ref, t_ref, v_ref, x_ref):
    blocks, h, _ = g_ref.shape
    row = lax.broadcasted_iota(jnp.int32, (h, h), 0)
    col = lax.broadcasted_iota(jnp.int32, (h, h), 1)
    for b in range(blocks):
        s = s_ref[b]
        back = narrow(s, s) * inv_n
        both = g_ref[b, :, h:]
        turned = both.T
        ident = jnp.where(row == col, ridge, 0.0)
        a_ref[b] = jnp.where(row >= col, both, turned) + back[:h, :h] + ident
        t_ref[b] = g_ref[b, :, :h] + back[h:, :h]
        v_ref[:, pl.ds(b * h, h)] = jnp.where(row < col, both, jnp.where(row == col, d_ref[b], turned)) + back[h:, h:] + ident
    invert([a_ref.at[b] for b in range(blocks)], [x_ref.at[b] for b in range(blocks)])


def tail_kernel(t_ref, v_ref, x_ref, a_ref, y_ref, o_ref):
    blocks, h, _ = t_ref.shape
    every = range(blocks)
    turns = []
    for b in every:
        t = t_ref[b]
        v = dot6(t, x_ref[b])
        turns.append(v)
        a_ref[b] = v_ref[:, pl.ds(b * h, h)] - lax.dot_general(v, t, (((1,), (1,)), ((), ())), precision=HI, preferred_element_type=f32)
    invert([a_ref.at[b] for b in every], [y_ref.at[b] for b in every])
    for b in every:
        v, y = turns[b], y_ref[b]
        low = dot6(y, v)
        o_ref[b, h:, h:] = y
        o_ref[b, h:, :h] = -low
        o_ref[b, :h, h:] = -low.T
        o_ref[b, :h, :h] = x_ref[b] + tdot6(v, low)


def head(g, d, s, n):
    shape = jax.ShapeDtypeStruct((g.shape[0], g.shape[1], g.shape[1]), f32)
    side = jax.ShapeDtypeStruct((g.shape[1], g.shape[0] * g.shape[1]), f32)
    _, t, v, x = call(functools.partial(head_kernel, 1.0 / n), 10, [shape, shape, side, shape], g, d, s)
    return t, v, x


def tail(t, v, x):
    blocks, h, _ = t.shape
    half = jax.ShapeDtypeStruct(t.shape, f32)
    return call(tail_kernel, 10, [half, half, jax.ShapeDtypeStruct((blocks, 2 * h, 2 * h), f32)], t, v, x)[2]


def pick(first, owner, own, other):
    return jnp.where(first, own, other) if owner == 0 else jnp.where(first, other, own)


def solve_kernel(inv_n, owned, core_ref, w_ref, w2_ref, x_ref, x2_ref, s_ref, s2_ref, t_ref, c_ref, c2_ref, f_ref, f2_ref, y_ref, o_ref, r_ref, d_ref, ts_ref, xv_ref, xv2_ref, sem):
    first = core_ref[0] == 0
    step = pl.program_id(0)
    copies = [pltpu.make_async_copy(x_ref, xv_ref, sem.at[0]), pltpu.make_async_copy(x2_ref, xv2_ref, sem.at[1])]

    def block(b):
        owner, local = b // owned, b % owned
        if b == 0:
            for copy in copies:
                copy.start()
            ts_ref[...] = t_ref[...]
            r_ref[...] = y_ref[...].astype(f32)
        if b == 1:
            for copy in copies:
                copy.wait()
        s = pick(first, owner, s_ref[local], s2_ref[local])
        ts = ts_ref[...]
        rhs = pick(first, owner, c_ref[0], c2_ref[0]) + narrow(s, ts) * inv_n
        for c in range(b):
            index, keeper = PAIRS[(b, c)]
            dims = (((0,), (0,)), ((), ())) if (keeper == 1 and index > 0) else (((1,), (0,)), ((), ()))
            hi, lo = split(pick(first, keeper, xv_ref[index], xv2_ref[index]))
            rhs = rhs - (
                lax.dot_general(hi, d_ref[c], dims, preferred_element_type=f32)
                + lax.dot_general(lo, d_ref[c], dims, preferred_element_type=f32)
            )
        delta = dot3(pick(first, owner, w_ref[0], w2_ref[0]), rhs)
        rounded = delta.astype(bf16)
        o_ref[0] = delta
        d_ref[b] = rounded
        sh, sl, sm = thirds(s)
        ts_ref[...] = ts - (dot1(sh, rounded) + (dot1(sl, rounded) + dot1(sm, rounded)))
        r_ref[...] -= dot1(pick(first, owner, f_ref[0], f2_ref[0]), rounded)

    for b in range(2 * owned):
        pl.when(step == b)(functools.partial(block, b))


def solve(core, w, w2, x, x2, s, s2, t, c, c2, f, f2, y, n):
    owned, width, columns = c.shape
    blocks = 2 * owned
    rows = f.shape[1]
    whole = lambda a: pl.BlockSpec(a.shape, lambda b: (0,) * a.ndim)
    local = lambda a: pl.BlockSpec((1,) + a.shape[1:], lambda b: (b % owned, 0, 0))
    anywhere = pl.BlockSpec(memory_space=pl.ANY)
    return pl.pallas_call(
        functools.partial(solve_kernel, 1.0 / n, owned),
        grid=(blocks,),
        in_specs=[pl.BlockSpec(memory_space=pltpu.SMEM), local(w), local(w2), anywhere, anywhere, whole(s), whole(s2)]
        + [whole(t), local(c), local(c2), local(f), local(f2), whole(y)],
        out_specs=[
            pl.BlockSpec((1, width, columns), lambda b: (b, 0, 0)),
            pl.BlockSpec((rows, columns), lambda b: (0, 0)),
        ],
        out_shape=[jax.ShapeDtypeStruct((blocks, width, columns), f32), jax.ShapeDtypeStruct((rows, columns), f32)],
        scratch_shapes=[
            pltpu.VMEM((blocks, width, columns), bf16),
            pltpu.VMEM(t.shape, f32),
            pltpu.VMEM(x.shape, f32),
            pltpu.VMEM(x2.shape, f32),
            pltpu.SemaphoreType.DMA((2,)),
        ],
        compiler_params=pltpu.CompilerParams(vmem_limit_bytes=40 * MIB),
        cost_estimate=cost(15),
        name="solve",
    )(core.reshape(1), w, w2, x, x2, s, s2, t, c, c2, f, f2, y)


PAIRS = {(1, 0): (0, 0), (2, 0): (1, 0), (3, 1): (2, 0), (3, 2): (0, 1), (2, 1): (1, 1), (3, 0): (2, 1)}


def tie(x, *after):
    for one in after:
        rows = min(x.shape[0], one.shape[0])
        zero = (one[:rows].astype(f32) * 0.0).astype(x.dtype)
        x = x + jnp.pad(zero, ((0, x.shape[0] - rows), (0, 0)))
    return x


ORDERS = ((0, 2, 1), (1, 2, 0), (0, 1, 2), (2, 0, 1))


class Chain:
    def __init__(self, x, order, scale):
        self.x, self.order, self.scale = x, order, scale
        self.step = 0
        self.extra = None

    def run(self, *after):
        count = len(self.order)
        halving = self.step < count
        bit = self.order[self.step if halving else 2 * count - 1 - self.step]
        mine = (lax.axis_index("rows") >> bit) & 1
        pairs = [(i, i ^ (1 << bit)) for i in range(lax.axis_size("rows"))]
        if halving:
            half = self.x.shape[0] // 2
            send = lax.dynamic_slice_in_dim(self.x, (1 - mine) * half, half)
            keep = lax.dynamic_slice_in_dim(self.x, mine * half, half)
            send = tie(send * self.scale, *after).astype(wire)
            self.got = got = lax.ppermute(send, "rows", pairs)
            self.x = keep + got.astype(f32) * (1.0 / self.scale)
        else:
            if self.step == count:
                self.x = (self.x * self.scale).astype(wire)
                if self.extra is not None:
                    self.x = jnp.concatenate([self.x, self.extra])
            x = tie(self.x, *after)
            self.got = got = lax.ppermute(x, "rows", pairs)
            self.x = jnp.where(mine == 1, jnp.concatenate([got, x]), jnp.concatenate([x, got]))
        self.step += 1

    def done(self):
        return self.step == 2 * len(self.order)


def groups(low):
    parts = lax.axis_size("rows")
    near = [[i + j for j in range(low)] for i in range(0, parts, low)]
    far = [[i + j for j in range(0, parts, low)] for i in range(low)]
    return near, far


def scatter_sum(x, scale, cut):
    x = (x * scale).astype(wire).reshape(len(cut[0]), -1, x.shape[-1])
    x = lax.all_to_all(x, "rows", 0, 0, axis_index_groups=cut)
    return jnp.sum(x.astype(f32), axis=0) * (1.0 / scale)


def swap(x):
    cores = lax.axis_size("blk")
    return lax.ppermute(x, "blk", [(i, (i + 1) % cores) for i in range(cores)])


def body(inputs, proj, phase, targets):
    parts = lax.axis_size("rows")
    core = lax.axis_index("blk")
    n = inputs.shape[0]
    columns = targets.shape[1]
    owned, _, width = proj.shape
    h = width // 2
    scale = 1.0 / math.sqrt(n * parts)
    gscale = 2.0**15
    cscale = 2.0 ** math.floor(math.log2(65504.0 / (8.0 * math.sqrt(n * parts))))
    bits = list(range(parts.bit_length() - 1))
    order_a, order_b, order_c, order_d = ([order[i] for i in range(min(3, len(bits)))] + bits[3:] for order in ORDERS)

    proj2, phase2 = swap(proj), swap(phase)
    shape = lambda *dims: jax.ShapeDtypeStruct(dims, f32)
    feats = jax.ShapeDtypeStruct((owned, n, width), bf16)
    sums, corrs = shape(owned, 1, width), shape(owned * width, columns)
    first = [feats, sums, shape(1, columns), shape(owned * h, width), shape(owned, 1, h), corrs]
    place = lambda space: pl.BlockSpec(memory_space=space)
    outs = first + [feats, sums, corrs, shape(3 * width, width)]
    moved = [inputs, proj, proj2, targets]
    own, own_sum, tsum, packed, corner, c, other, other_sum, c2, cross = pl.pallas_call(
        functools.partial(prelude_kernel, scale),
        in_specs=[place(pltpu.SMEM)] + [place(space) for space in (pl.ANY, pl.ANY, pltpu.VMEM, pl.ANY, pltpu.VMEM, pl.ANY)],
        out_specs=[pl.BlockSpec(o.shape) if o.dtype == bf16 else place(pltpu.VMEM) for o in outs],
        out_shape=outs,
        scratch_shapes=[pltpu.VMEM(a.shape, a.dtype) for a in moved] + [pltpu.SemaphoreType.DMA((len(moved),))],
        compiler_params=pltpu.CompilerParams(vmem_limit_bytes=52 * MIB),
        cost_estimate=cost(14),
        name="prelude",
    )(core.reshape(1), inputs, proj, phase, proj2, phase2, targets)
    corr1 = Chain(c, order_b, cscale)
    corr1.run()
    extra = jnp.concatenate([own_sum[:, 0], corner.reshape(-1, width) * gscale, tsum.reshape(-1, width)])
    high = extra.astype(wire)
    extra = jnp.concatenate([high, (extra - high.astype(f32)).astype(wire)])
    near, far = groups(min(4, parts))
    gram = scatter_sum(scatter_sum(packed, gscale, near), gscale, far)

    corr2 = Chain(c2, order_c, cscale)
    cross = Chain(cross, order_d, gscale)
    corr2.run()
    cross.run()
    piece, count = gram.shape[0], extra.shape[0] // 2
    gram = jnp.concatenate([(gram * gscale).astype(wire), extra])
    me = lax.axis_index("rows")
    for bit in bits[2:] + bits[:2]:
        got = lax.ppermute(gram, "rows", [(i, i ^ (1 << bit)) for i in range(parts)])
        gram = jnp.where((me >> bit) & 1 == 1, jnp.concatenate([got, gram]), jnp.concatenate([gram, got]))
    got = gram.reshape(parts, -1, width)
    extra = got[:, piece : piece + count].astype(f32) + got[:, piece + count :].astype(f32)
    g = got[:, :piece].reshape(owned, h, width).astype(f32) * (1.0 / gscale)
    s = extra[:, :owned].transpose(1, 0, 2)
    d = jnp.sum(extra[:, owned : owned + owned * h // width], axis=0).reshape(owned, 1, h) * (1.0 / gscale)
    ts = extra[:, owned + owned * h // width :].reshape(parts, columns)
    s2 = swap(s)
    bulk = (cross, corr1, corr2)
    for chain in bulk[1:]:
        while chain.step < 3:
            chain.run()
    g = tie(g.reshape(-1, width), corr1.got, corr2.got).reshape(g.shape)
    t, v, x = head(g, d, s, n)
    for chain in bulk[1:]:
        while chain.step < 4:
            chain.run()
    w = tail(t, tie(v, corr1.got, corr2.got), x)
    w2 = swap(w)
    half = len(bits)
    for chain in bulk:
        while not chain.done():
            chain.run(*{half + 1: (v,), half + 2: (w.reshape(-1, width),)}.get(chain.step, ()))
            if chain.step == 2 * half - 1:
                chain.third = chain.got
    cross.x = tie(cross.x, corr1.got, corr2.got)
    x2 = swap(cross.x)
    wide = lambda a, by: a.reshape(-1, width, a.shape[-1]).astype(f32) * (1.0 / by)
    c, c2 = wide(corr1.x, cscale), wide(corr2.x, cscale)
    return tuple(solve(core, w, w2, wide(cross.x, gscale), wide(x2, gscale), s, s2, ts, c, c2, own, other, targets, n))


def solution(mesh):
    return jax.shard_map(
        body,
        mesh=mesh,
        in_specs=(P("rows", None), P("blk", None, None), P("blk", None), P("rows", "blk")),
        out_specs=(P(None, None, "blk"), P("rows", "blk")),
        check_vma=False,
    )
```

```python
import functools
import math

import jax
import jax.numpy as jnp
from jax import lax
from jax.experimental import pallas as pl
from jax.experimental.pallas import tpu as pltpu
from jax.sharding import PartitionSpec as P

ridge = 0.05
wire = jnp.float16
HI = lax.Precision.HIGHEST
f32, bf16 = jnp.float32, jnp.bfloat16

SIN = (6.283185280262748, -41.341680654656756, 81.60247856840721, -76.58120078779972, 39.75982743860689)
MIB = 1024 * 1024


def cosine(x, scale):
    turns = x * (0.5 / math.pi)
    w = 0.25 - jnp.abs(turns - jnp.round(turns))
    u = w * w
    p = SIN[4] * scale
    for c in SIN[3::-1]:
        p = p * u + c * scale
    return w * p


def features(scale, x_ref, w_ref, p_ref, f_ref, s_ref):
    rows = x_ref.shape[0]
    tile = min(rows, 256)
    for b in range(w_ref.shape[0]):
        total = 0.0
        for i in range(rows // tile):
            at = pl.ds(i * tile, tile)
            pre = dot1(x_ref[at], w_ref[b]) + p_ref[...].astype(f32)[b : b + 1]
            out = cosine(pre, scale).astype(bf16)
            f_ref[b, at] = out
            total = total + jnp.sum(out.astype(f32), axis=0, keepdims=True)
        s_ref[b] = total


def tdot(a, b):
    return lax.dot_general(a, b, (((0,), (0,)), ((), ())), preferred_element_type=f32)


def outer(a, b):
    return jnp.broadcast_to(a, (128, a.shape[1])).T[:, :1] * b


def own_products(scale, x_ref, w_ref, p_ref, t_ref, f_ref, s_ref, ts_ref, g_ref, d_ref, c_ref):
    rows = x_ref.shape[0]
    blocks, _, width = w_ref.shape
    h = width // 2
    features(scale, x_ref, w_ref, p_ref, f_ref, s_ref)
    ts = jnp.sum(t_ref[...].astype(f32), axis=0, keepdims=True)
    ts_ref[...] = ts
    row = lax.broadcasted_iota(jnp.int32, (h, h), 0)
    col = lax.broadcasted_iota(jnp.int32, (h, h), 1)
    for b in range(blocks):
        low, high = f_ref[b, :, :h], f_ref[b, :, h:]
        turned = f_ref[b].T
        s = s_ref[b]
        back = outer(s, s) * (1.0 / rows)
        corner = dot1(turned[h:], high) - back[h:, h:]
        at = pl.ds(b * h, h)
        g_ref[at, h:] = jnp.where(row >= col, dot1(turned[:h], low) - back[:h, :h], corner)
        g_ref[at, :h] = dot1(turned[h:], low) - back[h:, :h]
        d_ref[b] = jnp.sum(jnp.where(row == col, corner, 0.0), axis=0, keepdims=True)
        c_ref[pl.ds(b * width, width)] = dot1(turned, t_ref[...]) - outer(s, ts) * (1.0 / rows)


def other_products(scale, core_ref, x_ref, w_ref, p_ref, t_ref, ts_ref, f_ref, s_ref, f2_ref, s2_ref, c_ref, x2_ref):
    rows = x_ref.shape[0]
    blocks, _, width = w_ref.shape
    features(scale, x_ref, w_ref, p_ref, f2_ref, s2_ref)
    for b in range(blocks):
        c_ref[pl.ds(b * width, width)] = tdot(f2_ref[b], t_ref[...]) - outer(s2_ref[b], ts_ref[...]) * (1.0 / rows)
    core = core_ref[0]
    made = ((f_ref, s_ref, 1, 0), (f2_ref, s2_ref, core, 0), (f2_ref, s2_ref, 1 - core, 1))
    for i, (feats, sums, left, right) in enumerate(made):
        product = tdot(feats[left], f_ref[right]) - outer(sums[left], s_ref[right]) * (1.0 / rows)
        x2_ref[pl.ds(i * width, width)] = product


def prelude_kernel(scale, core_ref, x_any, w_any, p_ref, w2_any, p2_ref, t_any, f_ref, s_ref, ts_ref, g_ref, d_ref, c_ref, f2_ref, s2_ref, c2_ref, x2_ref, x_ref, w_ref, w2_ref, t_ref, sem):
    moves = ((x_any, x_ref), (w_any, w_ref), (t_any, t_ref), (w2_any, w2_ref))
    copies = [pltpu.make_async_copy(source, to, sem.at[i]) for i, (source, to) in enumerate(moves)]
    for copy in copies:
        copy.start()
    for copy in copies[:3]:
        copy.wait()
    own_products(scale, x_ref, w_ref, p_ref, t_ref, f_ref, s_ref, ts_ref, g_ref, d_ref, c_ref)
    copies[3].wait()
    other_products(scale, core_ref, x_ref, w2_ref, p2_ref, t_ref, ts_ref, f_ref, s_ref, f2_ref, s2_ref, c2_ref, x2_ref)


def split(a):
    hi = a.astype(bf16)
    return hi, (a - hi.astype(f32)).astype(bf16)


def dot1(a, b):
    return jnp.dot(a, b, preferred_element_type=f32)


def dot3(a, b):
    ah, al = split(a)
    bh, bl = split(b)
    return dot1(ah, bh) + (dot1(ah, bl) + dot1(al, bh))


def dot6(a, b):
    return jnp.dot(a, b, precision=HI, preferred_element_type=f32)


def tdot6(a, b):
    return lax.dot_general(a, b, (((0,), (0,)), ((), ())), precision=HI, preferred_element_type=f32)


def thirds(a):
    hi, lo = split(a)
    return hi, lo, (a - hi.astype(f32) - lo.astype(f32)).astype(bf16)


def narrow(a, b):
    ah, am, al = thirds(a)
    bh, bm, bl = thirds(b)
    left = jnp.concatenate([al, ah, am, am, ah, ah])
    return lax.dot_general(left, jnp.concatenate([bh, bl, bm, bh, bm, bh]), (((0,), (0,)), ((), ())), preferred_element_type=f32)


def eye(n):
    return (lax.broadcasted_iota(jnp.int32, (n, n), 0) == lax.broadcasted_iota(jnp.int32, (n, n), 1)).astype(f32)


def invert(a_refs, x_refs):
    n = a_refs[0].shape[-1]
    top = jnp.float32(0.0)
    for a in a_refs:
        top = jnp.maximum(top, jnp.max(jnp.sum(jnp.abs(a[...]), axis=1)))
    top = top * 1.0001
    ident = eye(n)
    for x in x_refs:
        x[...] = ident * (1.0 / top)

    def step(low):
        scale = 2.0 / (1.0 + low)
        for a, x in zip(a_refs, x_refs):
            xv = x[...] * scale
            y = dot3(a[...], xv)
            x[...] = 2.0 * xv - dot3(xv, y)
        return jnp.minimum(4.0 * low / ((1.0 + low) * (1.0 + low)) * 0.999, 1.0)

    lax.while_loop(lambda low: low < 0.98, step, 0.9 * ridge / top)
    for a, x in zip(a_refs, x_refs):
        xv = x[...]
        x[...] = 2.0 * xv - dot6(xv, dot6(a[...], xv))


def cost(us):
    return pl.CostEstimate(flops=int(us * 1.15e9), bytes_accessed=0, transcendentals=0)


def call(kernel, us, out_shape, *args):
    return pl.pallas_call(
        kernel,
        out_shape=out_shape,
        cost_estimate=cost(us),
        compiler_params=pltpu.CompilerParams(vmem_limit_bytes=32 * MIB),
        name=kernel.func.__name__ if isinstance(kernel, functools.partial) else kernel.__name__,
    )(*args)


def head_kernel(inv_n, g_ref, d_ref, s_ref, a_ref, t_ref, v_ref, x_ref):
    blocks, h, _ = g_ref.shape
    row = lax.broadcasted_iota(jnp.int32, (h, h), 0)
    col = lax.broadcasted_iota(jnp.int32, (h, h), 1)
    for b in range(blocks):
        s = s_ref[b]
        back = narrow(s, s) * inv_n
        both = g_ref[b, :, h:]
        turned = both.T
        ident = jnp.where(row == col, ridge, 0.0)
        a_ref[b] = jnp.where(row >= col, both, turned) + back[:h, :h] + ident
        t_ref[b] = g_ref[b, :, :h] + back[h:, :h]
        v_ref[:, pl.ds(b * h, h)] = jnp.where(row < col, both, jnp.where(row == col, d_ref[b], turned)) + back[h:, h:] + ident
    invert([a_ref.at[b] for b in range(blocks)], [x_ref.at[b] for b in range(blocks)])


def tail_kernel(t_ref, v_ref, x_ref, a_ref, y_ref, o_ref):
    blocks, h, _ = t_ref.shape
    every = range(blocks)
    turns = []
    for b in every:
        t = t_ref[b]
        v = dot6(t, x_ref[b])
        turns.append(v)
        a_ref[b] = v_ref[:, pl.ds(b * h, h)] - lax.dot_general(v, t, (((1,), (1,)), ((), ())), precision=HI, preferred_element_type=f32)
    invert([a_ref.at[b] for b in every], [y_ref.at[b] for b in every])
    for b in every:
        v, y = turns[b], y_ref[b]
        low = dot6(y, v)
        o_ref[b, h:, h:] = y
        o_ref[b, h:, :h] = -low
        o_ref[b, :h, h:] = -low.T
        o_ref[b, :h, :h] = x_ref[b] + tdot6(v, low)


def head(g, d, s, n):
    shape = jax.ShapeDtypeStruct((g.shape[0], g.shape[1], g.shape[1]), f32)
    side = jax.ShapeDtypeStruct((g.shape[1], g.shape[0] * g.shape[1]), f32)
    _, t, v, x = call(functools.partial(head_kernel, 1.0 / n), 10, [shape, shape, side, shape], g, d, s)
    return t, v, x


def tail(t, v, x):
    blocks, h, _ = t.shape
    half = jax.ShapeDtypeStruct(t.shape, f32)
    return call(tail_kernel, 10, [half, half, jax.ShapeDtypeStruct((blocks, 2 * h, 2 * h), f32)], t, v, x)[2]


def pick(first, owner, own, other):
    return jnp.where(first, own, other) if owner == 0 else jnp.where(first, other, own)


def solve_kernel(inv_n, owned, core_ref, w_ref, w2_ref, x_ref, x2_ref, s_ref, s2_ref, t_ref, c_ref, c2_ref, f_ref, f2_ref, y_ref, o_ref, r_ref, d_ref, ts_ref, xv_ref, xv2_ref, sem):
    first = core_ref[0] == 0
    step = pl.program_id(0)
    copies = [pltpu.make_async_copy(x_ref, xv_ref, sem.at[0]), pltpu.make_async_copy(x2_ref, xv2_ref, sem.at[1])]

    def block(b):
        owner, local = b // owned, b % owned
        if b == 0:
            for copy in copies:
                copy.start()
            ts_ref[...] = t_ref[...]
            r_ref[...] = y_ref[...].astype(f32)
        if b == 1:
            for copy in copies:
                copy.wait()
        s = pick(first, owner, s_ref[local], s2_ref[local])
        ts = ts_ref[...]
        rhs = pick(first, owner, c_ref[0], c2_ref[0]) + narrow(s, ts) * inv_n
        for c in range(b):
            index, keeper = PAIRS[(b, c)]
            dims = (((0,), (0,)), ((), ())) if (keeper == 1 and index > 0) else (((1,), (0,)), ((), ()))
            hi, lo = split(pick(first, keeper, xv_ref[index], xv2_ref[index]))
            rhs = rhs - (
                lax.dot_general(hi, d_ref[c], dims, preferred_element_type=f32)
                + lax.dot_general(lo, d_ref[c], dims, preferred_element_type=f32)
            )
        delta = dot3(pick(first, owner, w_ref[0], w2_ref[0]), rhs)
        rounded = delta.astype(bf16)
        o_ref[0] = delta
        d_ref[b] = rounded
        sh, sl, sm = thirds(s)
        ts_ref[...] = ts - (dot1(sh, rounded) + (dot1(sl, rounded) + dot1(sm, rounded)))
        r_ref[...] -= dot1(pick(first, owner, f_ref[0], f2_ref[0]), rounded)

    for b in range(2 * owned):
        pl.when(step == b)(functools.partial(block, b))


def solve(core, w, w2, x, x2, s, s2, t, c, c2, f, f2, y, n):
    owned, width, columns = c.shape
    blocks = 2 * owned
    rows = f.shape[1]
    whole = lambda a: pl.BlockSpec(a.shape, lambda b: (0,) * a.ndim)
    local = lambda a: pl.BlockSpec((1,) + a.shape[1:], lambda b: (b % owned, 0, 0))
    anywhere = pl.BlockSpec(memory_space=pl.ANY)
    return pl.pallas_call(
        functools.partial(solve_kernel, 1.0 / n, owned),
        grid=(blocks,),
        in_specs=[pl.BlockSpec(memory_space=pltpu.SMEM), local(w), local(w2), anywhere, anywhere, whole(s), whole(s2)]
        + [whole(t), local(c), local(c2), local(f), local(f2), whole(y)],
        out_specs=[
            pl.BlockSpec((1, width, columns), lambda b: (b, 0, 0)),
            pl.BlockSpec((rows, columns), lambda b: (0, 0)),
        ],
        out_shape=[jax.ShapeDtypeStruct((blocks, width, columns), f32), jax.ShapeDtypeStruct((rows, columns), f32)],
        scratch_shapes=[
            pltpu.VMEM((blocks, width, columns), bf16),
            pltpu.VMEM(t.shape, f32),
            pltpu.VMEM(x.shape, f32),
            pltpu.VMEM(x2.shape, f32),
            pltpu.SemaphoreType.DMA((2,)),
        ],
        compiler_params=pltpu.CompilerParams(vmem_limit_bytes=40 * MIB),
        cost_estimate=cost(15),
        name="solve",
    )(core.reshape(1), w, w2, x, x2, s, s2, t, c, c2, f, f2, y)


PAIRS = {(1, 0): (0, 0), (2, 0): (1, 0), (3, 1): (2, 0), (3, 2): (0, 1), (2, 1): (1, 1), (3, 0): (2, 1)}


def tie(x, *after):
    for one in after:
        rows = min(x.shape[0], one.shape[0])
        zero = (one[:rows].astype(f32) * 0.0).astype(x.dtype)
        x = x + jnp.pad(zero, ((0, x.shape[0] - rows), (0, 0)))
    return x


ORDERS = ((0, 2, 1), (1, 2, 0), (0, 1, 2), (2, 0, 1))


class Chain:
    def __init__(self, x, order, scale):
        self.x, self.order, self.scale = x, order, scale
        self.step = 0
        self.extra = None

    def run(self, *after):
        count = len(self.order)
        halving = self.step < count
        bit = self.order[self.step if halving else 2 * count - 1 - self.step]
        mine = (lax.axis_index("rows") >> bit) & 1
        pairs = [(i, i ^ (1 << bit)) for i in range(lax.axis_size("rows"))]
        if halving:
            half = self.x.shape[0] // 2
            send = lax.dynamic_slice_in_dim(self.x, (1 - mine) * half, half)
            keep = lax.dynamic_slice_in_dim(self.x, mine * half, half)
            send = tie(send * self.scale, *after).astype(wire)
            self.got = got = lax.ppermute(send, "rows", pairs)
            self.x = keep + got.astype(f32) * (1.0 / self.scale)
        else:
            if self.step == count:
                self.x = (self.x * self.scale).astype(wire)
                if self.extra is not None:
                    self.x = jnp.concatenate([self.x, self.extra])
            x = tie(self.x, *after)
            self.got = got = lax.ppermute(x, "rows", pairs)
            self.x = jnp.where(mine == 1, jnp.concatenate([got, x]), jnp.concatenate([x, got]))
        self.step += 1

    def done(self):
        return self.step == 2 * len(self.order)


def groups(low):
    parts = lax.axis_size("rows")
    near = [[i + j for j in range(low)] for i in range(0, parts, low)]
    far = [[i + j for j in range(0, parts, low)] for i in range(low)]
    return near, far


def scatter_sum(x, scale, cut):
    x = (x * scale).astype(wire).reshape(len(cut[0]), -1, x.shape[-1])
    x = lax.all_to_all(x, "rows", 0, 0, axis_index_groups=cut)
    return jnp.sum(x.astype(f32), axis=0) * (1.0 / scale)


def swap(x):
    cores = lax.axis_size("blk")
    return lax.ppermute(x, "blk", [(i, (i + 1) % cores) for i in range(cores)])


def body(inputs, proj, phase, targets):
    parts = lax.axis_size("rows")
    core = lax.axis_index("blk")
    n = inputs.shape[0]
    columns = targets.shape[1]
    owned, _, width = proj.shape
    h = width // 2
    scale = 1.0 / math.sqrt(n * parts)
    gscale = 2.0**15
    cscale = 2.0 ** math.floor(math.log2(65504.0 / (8.0 * math.sqrt(n * parts))))
    bits = list(range(parts.bit_length() - 1))
    order_a, order_b, order_c, order_d = ([order[i] for i in range(min(3, len(bits)))] + bits[3:] for order in ORDERS)

    proj2, phase2 = swap(proj), swap(phase)
    shape = lambda *dims: jax.ShapeDtypeStruct(dims, f32)
    feats = jax.ShapeDtypeStruct((owned, n, width), bf16)
    sums, corrs = shape(owned, 1, width), shape(owned * width, columns)
    first = [feats, sums, shape(1, columns), shape(owned * h, width), shape(owned, 1, h), corrs]
    place = lambda space: pl.BlockSpec(memory_space=space)
    outs = first + [feats, sums, corrs, shape(3 * width, width)]
    moved = [inputs, proj, proj2, targets]
    own, own_sum, tsum, packed, corner, c, other, other_sum, c2, cross = pl.pallas_call(
        functools.partial(prelude_kernel, scale),
        in_specs=[place(pltpu.SMEM)] + [place(space) for space in (pl.ANY, pl.ANY, pltpu.VMEM, pl.ANY, pltpu.VMEM, pl.ANY)],
        out_specs=[pl.BlockSpec(o.shape) if o.dtype == bf16 else place(pltpu.VMEM) for o in outs],
        out_shape=outs,
        scratch_shapes=[pltpu.VMEM(a.shape, a.dtype) for a in moved] + [pltpu.SemaphoreType.DMA((len(moved),))],
        compiler_params=pltpu.CompilerParams(vmem_limit_bytes=52 * MIB),
        cost_estimate=cost(14),
        name="prelude",
    )(core.reshape(1), inputs, proj, phase, proj2, phase2, targets)
    corr1 = Chain(c, order_b, cscale)
    corr1.run()
    extra = jnp.concatenate([own_sum[:, 0], corner.reshape(-1, width) * gscale, tsum.reshape(-1, width)])
    high = extra.astype(wire)
    extra = jnp.concatenate([high, (extra - high.astype(f32)).astype(wire)])
    near, far = groups(min(4, parts))
    gram = scatter_sum(scatter_sum(packed, gscale, near), gscale, far)

    corr2 = Chain(c2, order_c, cscale)
    cross = Chain(cross, order_d, gscale)
    corr2.run()
    cross.run()
    piece, count = gram.shape[0], extra.shape[0] // 2
    gram = jnp.concatenate([(gram * gscale).astype(wire), extra])
    me = lax.axis_index("rows")
    for bit in bits[2:] + bits[:2]:
        got = lax.ppermute(gram, "rows", [(i, i ^ (1 << bit)) for i in range(parts)])
        gram = jnp.where((me >> bit) & 1 == 1, jnp.concatenate([got, gram]), jnp.concatenate([gram, got]))
    got = gram.reshape(parts, -1, width)
    extra = got[:, piece : piece + count].astype(f32) + got[:, piece + count :].astype(f32)
    g = got[:, :piece].reshape(owned, h, width).astype(f32) * (1.0 / gscale)
    s = extra[:, :owned].transpose(1, 0, 2)
    d = jnp.sum(extra[:, owned : owned + owned * h // width], axis=0).reshape(owned, 1, h) * (1.0 / gscale)
    ts = extra[:, owned + owned * h // width :].reshape(parts, columns)
    s2 = swap(s)
    bulk = (cross, corr1, corr2)
    for chain in bulk[1:]:
        while chain.step < 3:
            chain.run()
    g = tie(g.reshape(-1, width), corr1.got, corr2.got).reshape(g.shape)
    t, v, x = head(g, d, s, n)
    for chain in bulk[1:]:
        while chain.step < 4:
            chain.run()
    w = tail(t, tie(v, corr1.got, corr2.got), x)
    w2 = swap(w)
    half = len(bits)
    for chain in bulk:
        while not chain.done():
            chain.run(*{half + 1: (v,), half + 2: (w.reshape(-1, width),)}.get(chain.step, ()))
            if chain.step == 2 * half - 1:
                chain.third = chain.got
    cross.x = tie(cross.x, corr1.got, corr2.got)
    x2 = swap(cross.x)
    wide = lambda a, by: a.reshape(-1, width, a.shape[-1]).astype(f32) * (1.0 / by)
    c, c2 = wide(corr1.x, cscale), wide(corr2.x, cscale)
    return tuple(solve(core, w, w2, wide(cross.x, gscale), wide(x2, gscale), s, s2, ts, c, c2, own, other, targets, n))


def solution(mesh):
    return jax.shard_map(
        body,
        mesh=mesh,
        in_specs=(P("rows", None), P("blk", None, None), P("blk", None), P("rows", "blk")),
        out_specs=(P(None, None, "blk"), P("rows", "blk")),
        check_vma=False,
    )
```
